128 devices in a mesh: mp: 8 (over z_lo, x), feat: 16 (over y, z_hi, core).
Axes of the slice: x: 4, y: 4, z: 4 (z_hi: 2, z_lo: 2; z = z_hi * 2 + z_lo), core: 2. Of those that a mesh axis runs over, the one named last changes fastest.
Arguments:
- residual_in: bfloat16 [256, 3584], P(None, 'feat'), may hold values from -24 to 24
- norm_gain: float32 [3584], P('feat'), may hold values from 0.5 to 1.5
- gate_weight: bfloat16 [3584, 14336], P('feat', 'mp'), may hold values from -0.09375 to 0.09375
- up_weight: bfloat16 [3584, 14336], P('feat', 'mp'), may hold values from -0.09375 to 0.09375
- down_weight: bfloat16 [14336, 3584], P('mp', 'feat'), may hold values from -0.046875 to 0.046875
- encoder_weight: bfloat16 [3584, 65536], P(None, ('mp', 'feat')), may hold values from -0.375 to 0.375
- encoder_bias: float32 [65536], P(('mp', 'feat')), may hold values from -1.5 to 0.5
- decoder_weight: bfloat16 [65536, 3584], P(('mp', 'feat')), may hold values from -0.09375 to 0.09375
- decoder_bias: float32 [3584], replicated, may hold values from -3 to 3
Outputs:
- feature_codes: bfloat16 [256, 65536], P(None, ('mp', 'feat'))
- reconstruction: bfloat16 [256, 3584], P(('mp', 'feat'))
- encoder_gradient: bfloat16 [3584, 65536], P(None, ('mp', 'feat'))
- decoder_gradient: bfloat16 [65536, 3584], P(('mp', 'feat'))
- input_gradient: float32 [256, 3584], P(('mp', 'feat'))
The draws below stay inside these ranges and needn't reach their ends.
All inputs are finite; a program needn't handle non-finite values.
Results may differ from the reference program's by a relative error of at most 0.023.
Values may be sent and summed in bfloat16 or wider, within the bound.
No kernel may reach another device: no remote copies, remote signals or barrier semaphores. Data moves between devices by JAX's collectives and lax.ppermute only.
A program may use at most 128 MiB of HBM per device.

```python
import math
import jax
import jax.numpy as jnp
from jax import lax

D = 3584
FF = 14336
F = 65536
ROWS = 256


def draw_residual_in(key, part):
    key_base, key_columns, key_rows = jax.random.split(key, 3)
    position = jnp.arange(D, dtype=jnp.float32) / D
    column_scale = jnp.exp(math.log(3.0) * position + jax.random.uniform(key_columns, (D,), jnp.float32, 0.0, math.log(3.3)))
    values = jnp.clip(jax.random.normal(key_base, (ROWS, D), jnp.float32), -4.0, 4.0)
    row_scale = jnp.exp(jax.random.uniform(key_rows, (ROWS, 1), jnp.float32, math.log(0.3), math.log(3.0)))
    result = jnp.clip(0.35 * values * row_scale * column_scale[None, :], -24.0, 24.0)
    return result.astype(jnp.bfloat16)


def with_spikes(values, own_key, source, target, parts, factor):
    owner, partner = [(jnp.arange(values.shape[axis_at]) // (values.shape[axis_at] // parts)).reshape([-1 if axis == axis_at else 1 for axis in range(values.ndim)]) for axis_at in (source, target)]
    chosen = jax.random.permutation(own_key, parts)[partner]
    strong = (owner == chosen) | (owner == (partner + parts // 2) % parts)
    return jnp.where(strong, factor * values, values)


def steps_of(rng, shape, cuts, low, high):
    loudness = 1.0
    for axis_at, blocks in cuts:
        draws = jax.random.uniform(jax.random.fold_in(jax.random.fold_in(rng, 6), axis_at), (blocks,), jnp.float32, low / len(cuts), high / len(cuts))
        loudness = loudness * jnp.repeat(jnp.exp(draws), shape[axis_at] // blocks).reshape((-1,) + (1,) * (len(shape) - 1 - axis_at))
    return loudness


def scatter_about(key, dims, scale, reach, shards=(), kind=jnp.bfloat16):
    array = scale * jax.random.normal(key, dims, jnp.float32)
    if shards:
        array = array * steps_of(key, dims, shards, -0.22, 0.18)
    return jnp.clip(array, -reach, reach).astype(kind)


def noise_with(rng, extent, deviation, most, cuts, heavy, kind=jnp.bfloat16):
    array = deviation * jax.random.normal(rng, extent, jnp.float32)
    if cuts:
        array = array * steps_of(rng, extent, cuts, -0.22, 0.18)
    return jnp.clip(with_spikes(array, jax.random.fold_in(rng, 3), *heavy), -most, most).astype(kind)


def setup_inputs(seed: int = 0) -> dict:
    key_of = jax.random.split(jax.random.key(seed), 10)
    return {
        "residual_in": draw_residual_in(jax.random.fold_in(key_of[9], 71), 0),
        "norm_gain": jnp.clip(1.0 + 0.1 * jax.random.normal(key_of[1], (D,), jnp.float32), 0.5, 1.5),
        "gate_weight": scatter_about(key_of[2], (D, FF), D ** -0.5, 0.09375, ((0, 16), (1, 8))),
        "up_weight": scatter_about(key_of[3], (D, FF), D ** -0.5, 0.09375, ((0, 16), (1, 8))),
        "down_weight": scatter_about(key_of[4], (FF, D), FF ** -0.5, 0.046875, ((0, 8), (1, 16))),
        "encoder_weight": noise_with(key_of[5], (D, F), D ** -0.5, 0.375, ((1, 128),), (1, 0, 128, 5.5)),
        "encoder_bias": jnp.clip(-1.5 + 2.0 * jax.random.uniform(key_of[6], (F,), jnp.float32) ** steps_of(key_of[6], (F,), ((0, 128),), -0.2, 0.2), -1.5, 0.5),
        "decoder_weight": noise_with(key_of[7], (F, D), F ** -0.5, 0.09375, ((0, 128),), (0, 1, 128, 5.5)),
        "decoder_bias": scatter_about(key_of[8], (D,), 0.5, 3.0, (), jnp.float32),
    }


sparsity_weight = 0.2
norm_eps = 1e-06

def reference(residual_in, norm_gain, gate_weight, up_weight, down_weight, encoder_weight, encoder_bias, decoder_weight, decoder_bias):
    source = residual_in.astype(jnp.float32)
    inverse_scale = lax.rsqrt(lax.optimization_barrier(jnp.mean(source * source, axis=1, keepdims=True)) + norm_eps)
    normed = (source * inverse_scale * norm_gain[None, :]).astype(jnp.bfloat16)
    gate = jnp.dot(normed, gate_weight, preferred_element_type=jnp.float32)
    upward = jnp.dot(normed, up_weight, preferred_element_type=jnp.float32)
    hidden = (jax.nn.silu(gate) * upward).astype(jnp.bfloat16)
    mixed = jnp.dot(hidden, down_weight, preferred_element_type=jnp.float32)
    stream = (source + mixed).astype(jnp.bfloat16)
    encoded = jnp.dot(stream, encoder_weight, preferred_element_type=jnp.float32) + encoder_bias[None, :]
    feature_codes = jax.nn.softplus(encoded).astype(jnp.bfloat16)
    recon_full = jnp.dot(feature_codes, decoder_weight, preferred_element_type=jnp.float32) + decoder_bias[None, :]
    error = (recon_full - stream.astype(jnp.float32)).astype(jnp.bfloat16)
    decoder_gradient = jnp.dot(feature_codes.T, error, preferred_element_type=jnp.float32).astype(jnp.bfloat16)
    code_gradient = jnp.dot(error, decoder_weight.T, preferred_element_type=jnp.float32)
    encoded_gradient = (jax.nn.sigmoid(encoded) * (code_gradient + sparsity_weight)).astype(jnp.bfloat16)
    encoder_gradient = jnp.dot(stream.T, encoded_gradient, preferred_element_type=jnp.float32).astype(jnp.bfloat16)
    input_gradient = jnp.dot(encoded_gradient, encoder_weight.T, preferred_element_type=jnp.float32) - error.astype(jnp.float32)
    return (feature_codes, recon_full.astype(jnp.bfloat16), encoder_gradient, decoder_gradient, input_gradient)
```

```python
import jax
import jax.numpy as jnp
from jax import lax
from jax.sharding import Mesh
from jax.sharding import PartitionSpec as P

D = 3584
ROWS = 256
HALF = ROWS // 2
CHIPS = 64

MP = ("zl", "x")
RING = ("y", "zh")
FEAT = RING + ("c",)
CHIP = MP + RING
ALL = MP + FEAT

sparsity_weight = 0.2
norm_eps = 1e-06
bf16 = jnp.bfloat16
f32 = jnp.float32


def dot(a, b, ca, cb):
    return lax.dot_general(a, b, (((ca,), (cb,)), ((), ())), preferred_element_type=f32)


def swap(v):
    return lax.ppermute(v, "c", [(0, 1), (1, 0)])


def scatter_sum(v, axes, parts):
    arrived = swap(v[HALF:].astype(bf16))
    both = (v[:HALF].astype(f32) + arrived.astype(f32)).astype(bf16)
    both = both.reshape(parts, HALF // parts, v.shape[1])
    both = lax.all_to_all(both, axes, 0, 0, tiled=True)
    return jnp.sum(both.astype(f32), axis=0)


def gather_rows(v, axes, parts):
    copies = jnp.broadcast_to(v[None], (parts,) + v.shape)
    own = lax.all_to_all(copies, axes, 0, 0, tiled=True).reshape(HALF, v.shape[1])
    return jnp.concatenate([own, swap(own)], axis=0)


def shards(
    residual_in,
    norm_gain,
    gate_weight,
    up_weight,
    down_weight,
    encoder_weight,
    encoder_bias,
    decoder_weight,
    decoder_bias,
):
    hidden_local = gate_weight.shape[1]
    core = lax.axis_index("c")
    at = lax.broadcasted_iota(jnp.int32, (ROWS, ROWS), 0)
    row = lax.broadcasted_iota(jnp.int32, (ROWS, ROWS), 1)
    inside = at % HALF
    wanted = (inside // 2) * 4 + ((at // HALF) ^ core) * 2 + inside % 2
    order = (row == wanted).astype(bf16)

    source = dot(order, residual_in, 1, 0)
    squares = jnp.sum(source * source, axis=1)
    scaled = (source * norm_gain[None, :]).astype(bf16)

    def three(v):
        hi = v.astype(bf16)
        mid = (v - hi.astype(f32)).astype(bf16)
        lo = (v - hi.astype(f32) - mid.astype(f32)).astype(bf16)
        return jnp.stack([hi, mid, lo], axis=-1)

    joint_weight = jnp.concatenate([gate_weight, up_weight], axis=1)
    partial = dot(scaled, joint_weight, 1, 0).astype(bf16)
    squares_both = squares[:HALF] + swap(squares[HALF:])
    arrived = swap(partial[HALF:])
    both = (partial[:HALF].astype(f32) + arrived.astype(f32)).astype(bf16)
    both = jnp.concatenate([both, jnp.pad(three(squares_both), ((0, 0), (0, 125)))], axis=1)
    both = lax.all_to_all(both.reshape(8, 16, both.shape[1]), RING, 0, 0, tiled=True)
    projected = jnp.sum(both.astype(f32), axis=0)
    mean = jnp.sum(projected[:, 2 * hidden_local :], axis=1, keepdims=True) / D
    projected = projected[:, : 2 * hidden_local] * lax.rsqrt(mean + norm_eps)
    hidden = (jax.nn.silu(projected[:, :hidden_local]) * projected[:, hidden_local:]).astype(bf16)

    hidden_all = gather_rows(hidden, RING, 8)
    partial_mixed = (dot(hidden_all, down_weight, 1, 0) + source * 0.125).astype(bf16)
    other = swap(partial_mixed[HALF:])
    own = partial_mixed[:HALF]
    first = jnp.where(core == 0, own, other)
    second = jnp.where(core == 0, other, own)
    columns = jnp.stack([first.reshape(CHIPS, 2, -1), second.reshape(CHIPS, 2, -1)], axis=1)
    columns = lax.all_to_all(columns, CHIP, 0, 0, tiled=True)
    columns = jnp.sum(columns.reshape(8, 8, 2, 2, -1).astype(f32), axis=0)
    stream_own = columns.transpose(2, 0, 1, 3).reshape(2, D).astype(bf16)
    stream = gather_rows(stream_own, CHIP, CHIPS)

    encoded = dot(stream, encoder_weight, 1, 0) + encoder_bias[None, :]
    feature_codes = jax.nn.softplus(encoded).astype(bf16)
    recon_own = scatter_sum(dot(feature_codes, decoder_weight, 1, 0), CHIP, CHIPS) + decoder_bias[None, :]
    error_own = (recon_own - stream_own.astype(f32)).astype(bf16)
    error = gather_rows(error_own, CHIP, CHIPS)
    code_gradient = dot(error, decoder_weight, 1, 1)
    encoded_gradient = (jax.nn.sigmoid(encoded) * (code_gradient + sparsity_weight)).astype(bf16)
    input_gradient = scatter_sum(
        dot(encoded_gradient, encoder_weight, 1, 1), CHIP, CHIPS
    ) - error_own.astype(f32)
    decoder_gradient = dot(feature_codes, error, 0, 0).astype(bf16)
    encoder_gradient = dot(stream, encoded_gradient, 0, 0).astype(bf16)
    codes_out = dot(order, feature_codes, 0, 0).astype(bf16)
    return codes_out, recon_own.astype(bf16), encoder_gradient, decoder_gradient, input_gradient


def solution(mesh):
    fine = Mesh(mesh.devices.reshape(2, 4, 4, 2, 2), ("zl", "x", "y", "zh", "c"))
    in_specs = (
        P(None, FEAT),
        P(FEAT),
        P(FEAT, MP),
        P(FEAT, MP),
        P(MP, FEAT),
        P(None, ALL),
        P(ALL),
        P(ALL, None),
        P(),
    )
    out_specs = (P(None, ALL), P(ALL, None), P(None, ALL), P(ALL, None), P(ALL, None))
    return jax.shard_map(shards, mesh=fine, in_specs=in_specs, out_specs=out_specs, check_vma=False)
```

```python
import jax
import jax.numpy as jnp
from jax import lax
from jax.sharding import Mesh
from jax.sharding import PartitionSpec as P

D = 3584
ROWS = 256
HALF = ROWS // 2
CHIPS = 64

MP = ("zl", "x")
RING = ("y", "zh")
FEAT = RING + ("c",)
CHIP = MP + RING
ALL = MP + FEAT

sparsity_weight = 0.2
norm_eps = 1e-06
bf16 = jnp.bfloat16
f32 = jnp.float32


def dot(a, b, ca, cb):
    return lax.dot_general(a, b, (((ca,), (cb,)), ((), ())), preferred_element_type=f32)


def swap(v):
    return lax.ppermute(v, "c", [(0, 1), (1, 0)])


def exchange(v, axes):
    return lax.all_to_all(v, axes, 0, 0, tiled=True)


def copies_to(v, axes, parts):
    return exchange(jnp.broadcast_to(v[None], (parts,) + v.shape), axes)


def three(v):
    hi = v.astype(bf16)
    mid = (v - hi.astype(f32)).astype(bf16)
    lo = (v - hi.astype(f32) - mid.astype(f32)).astype(bf16)
    return jnp.stack([hi, mid, lo], axis=-1)


def shards(
    residual_in,
    norm_gain,
    gate_weight,
    up_weight,
    down_weight,
    encoder_weight,
    encoder_bias,
    decoder_weight,
    decoder_bias,
):
    hidden_local = gate_weight.shape[1]
    core = lax.axis_index("c")

    def by_core(zero, one):
        return jnp.where(core == 0, zero, one)

    at = lax.broadcasted_iota(jnp.int32, (ROWS, ROWS), 0)
    row = lax.broadcasted_iota(jnp.int32, (ROWS, ROWS), 1)
    inside = at % HALF
    order = (row == (inside // 2) * 4 + (at // HALF) * 2 + inside % 2).astype(bf16)
    keep_order = by_core(order[:HALF], order[HALF:])
    send_order = by_core(order[HALF:], order[:HALF])

    joint_weight = jnp.concatenate([gate_weight, up_weight], axis=1)

    def project(rows):
        source = dot(rows, residual_in, 1, 0)
        squares = jnp.sum(source * source, axis=1)
        return dot((source * norm_gain[None, :]).astype(bf16), joint_weight, 1, 0), squares

    sent, squares_sent = project(send_order)
    arrived, squares_arrived = swap(sent.astype(bf16)), swap(squares_sent)
    kept, squares_kept = project(keep_order)
    both = (kept + arrived.astype(f32)).astype(bf16)
    both = jnp.concatenate([both, jnp.pad(three(squares_kept + squares_arrived), ((0, 0), (0, 125)))], axis=1)
    both = exchange(both.reshape(8, 16, both.shape[1]), RING)
    projected = jnp.sum(both.astype(f32), axis=0)
    mean = jnp.sum(projected[:, 2 * hidden_local :], axis=1, keepdims=True) / D
    projected = projected[:, : 2 * hidden_local] * lax.rsqrt(mean + norm_eps)
    hidden = (jax.nn.silu(projected[:, :hidden_local]) * projected[:, hidden_local:]).astype(bf16)

    hidden_kept = copies_to(hidden, RING, 8).reshape(HALF, hidden_local)
    hidden_other = swap(hidden_kept)
    mixed_kept = dot(down_weight, hidden_kept, 0, 1).astype(bf16)
    mixed_other = dot(down_weight, hidden_other, 0, 1).astype(bf16)
    mixed = by_core(
        jnp.concatenate([mixed_kept, mixed_other], axis=1),
        jnp.concatenate([mixed_other, mixed_kept], axis=1),
    )
    mixed = jnp.sum(copies_to(mixed, MP, 8).astype(f32), axis=0)
    stream_cols = (dot(residual_in, order, 0, 1) + mixed).astype(bf16)

    blocks_kept = copies_to(stream_cols, RING, 8)
    blocks_other = swap(blocks_kept)
    encoder_blocks = encoder_weight.reshape(8, 2, D // 16, -1)
    encoder_kept = by_core(encoder_blocks[:, 0], encoder_blocks[:, 1]).reshape(D // 2, -1)
    encoder_other = by_core(encoder_blocks[:, 1], encoder_blocks[:, 0]).reshape(D // 2, -1)
    encoded = (
        dot(blocks_kept.reshape(D // 2, ROWS), encoder_kept, 0, 0)
        + dot(blocks_other.reshape(D // 2, ROWS), encoder_other, 0, 0)
        + encoder_bias[None, :]
    )
    codes = jax.nn.softplus(encoded).astype(bf16)
    codes_kept = by_core(codes[:HALF], codes[HALF:])
    codes_other = by_core(codes[HALF:], codes[:HALF])

    arrived = swap(dot(codes_other, decoder_weight, 1, 0).astype(bf16))
    both = (dot(codes_kept, decoder_weight, 1, 0) + arrived.astype(f32)).astype(bf16)
    recon_own = jnp.sum(exchange(both.reshape(CHIPS, 2, D), CHIP).astype(f32), axis=0) + decoder_bias[None, :]

    stream = by_core(
        jnp.stack([blocks_kept, blocks_other], axis=1),
        jnp.stack([blocks_other, blocks_kept], axis=1),
    ).reshape(D, ROWS)
    chip = lax.axis_index(CHIP)
    own = core * HALF + chip * 2 + lax.broadcasted_iota(jnp.int32, (2, ROWS), 0)
    own = (lax.broadcasted_iota(jnp.int32, (2, ROWS), 1) == own).astype(bf16)
    stream_own = dot(own, stream, 1, 1)
    codes_out = dot(order, codes, 0, 0).astype(bf16)

    error_own = (recon_own - stream_own).astype(bf16)
    error_kept = copies_to(error_own, CHIP, CHIPS).reshape(HALF, D)
    error_other = swap(error_kept)
    slope = jax.nn.sigmoid(encoded)
    slope_kept = by_core(slope[:HALF], slope[HALF:])
    slope_other = by_core(slope[HALF:], slope[:HALF])
    grad_kept = (slope_kept * (dot(error_kept, decoder_weight, 1, 1) + sparsity_weight)).astype(bf16)
    grad_other = (slope_other * (dot(error_other, decoder_weight, 1, 1) + sparsity_weight)).astype(bf16)
    arrived = swap(dot(grad_other, encoder_weight, 1, 1).astype(bf16))
    both = (dot(grad_kept, encoder_weight, 1, 1) + arrived.astype(f32)).astype(bf16)
    input_gradient = jnp.sum(
        exchange(both.reshape(CHIPS, 2, D), CHIP).astype(f32), axis=0
    ) - error_own.astype(f32)

    decoder_gradient = dot(
        jnp.concatenate([codes_kept, codes_other], axis=0),
        jnp.concatenate([error_kept, error_other], axis=0),
        0,
        0,
    ).astype(bf16)
    grad = by_core(
        jnp.concatenate([grad_kept, grad_other], axis=0),
        jnp.concatenate([grad_other, grad_kept], axis=0),
    )
    encoder_gradient = dot(stream, grad, 1, 0).astype(bf16)
    return codes_out, recon_own.astype(bf16), encoder_gradient, decoder_gradient, input_gradient


def solution(mesh):
    fine = Mesh(mesh.devices.reshape(2, 4, 4, 2, 2), ("zl", "x", "y", "zh", "c"))
    in_specs = (
        P(None, FEAT),
        P(FEAT),
        P(FEAT, MP),
        P(FEAT, MP),
        P(MP, FEAT),
        P(None, ALL),
        P(ALL),
        P(ALL, None),
        P(),
    )
    out_specs = (P(None, ALL), P(ALL, None), P(None, ALL), P(ALL, None), P(ALL, None))
    return jax.shard_map(shards, mesh=fine, in_specs=in_specs, out_specs=out_specs, check_vma=False)
```

```python
import jax
import jax.numpy as jnp
from jax import lax
from jax.sharding import Mesh
from jax.sharding import PartitionSpec as P

D = 3584
ROWS = 256
HALF = D // 2
CHIPS = 64

MP = ("zl", "x")
RING = ("y", "zh")
FEAT = RING + ("c",)
CHIP = MP + RING
ALL = MP + FEAT

sparsity_weight = 0.2
norm_eps = 1e-06
bf16 = jnp.bfloat16
f32 = jnp.float32


def dot(a, b, ca, cb):
    return lax.dot_general(a, b, (((ca,), (cb,)), ((), ())), preferred_element_type=f32)


def swap(v):
    return lax.ppermute(v, "c", [(0, 1), (1, 0)])


def exchange(v, axes):
    return lax.all_to_all(v, axes, 0, 0, tiled=True)


def copies_to(v, axes, parts):
    return exchange(jnp.broadcast_to(v[None], (parts,) + v.shape), axes)


def halves(v, core, axis):
    size = v.shape[axis] // 2
    return (
        lax.dynamic_slice_in_dim(v, core * size, size, axis),
        lax.dynamic_slice_in_dim(v, (1 - core) * size, size, axis),
    )


def shards(
    residual_in,
    norm_gain,
    gate_weight,
    up_weight,
    down_weight,
    encoder_weight,
    encoder_bias,
    decoder_weight,
    decoder_bias,
):
    core = lax.axis_index("c")
    chip = lax.axis_index(CHIP)

    def joined(kept, other, axis):
        return jnp.where(
            core == 0,
            jnp.concatenate([kept, other], axis=axis),
            jnp.concatenate([other, kept], axis=axis),
        )

    source = residual_in.astype(f32)
    scaled = (source * norm_gain[None, :]).astype(bf16)
    gate_kept, gate_other = halves(gate_weight, core, 1)
    up_kept, up_other = halves(up_weight, core, 1)
    hidden_half = gate_kept.shape[1]
    squared = source * source
    high = squared.astype(bf16)
    low = (squared - high.astype(f32)).astype(bf16)
    ones = jnp.ones((source.shape[1], 128), bf16)
    squares = dot(high, ones, 1, 0) + dot(low, ones, 1, 0)

    sent = jnp.concatenate([dot(scaled, gate_other, 1, 0), dot(scaled, up_other, 1, 0)], axis=1)
    arrived, squares_arrived = swap(sent.astype(bf16)), swap(squares)
    both = jnp.concatenate([dot(scaled, gate_kept, 1, 0), dot(scaled, up_kept, 1, 0)], axis=1)
    both = (both + arrived.astype(f32)).astype(bf16)
    squares = squares + squares_arrived
    first = squares.astype(bf16)
    second = (squares - first.astype(f32)).astype(bf16)
    third = (squares - first.astype(f32) - second.astype(f32)).astype(bf16)
    lane = lax.broadcasted_iota(jnp.int32, squares.shape, 1)
    parts = jnp.where(lane == 0, first, jnp.where(lane == 1, second, jnp.where(lane == 2, third, 0)))
    both = jnp.concatenate([both, parts.astype(bf16)], axis=1)
    both = exchange(both.reshape(8, 32, both.shape[1]), RING)
    projected = jnp.sum(both.astype(f32), axis=0)
    mean = jnp.sum(projected[:, 2 * hidden_half :], axis=1, keepdims=True) / D
    projected = projected[:, : 2 * hidden_half] * lax.rsqrt(mean + norm_eps)
    hidden = (jax.nn.silu(projected[:, :hidden_half]) * projected[:, hidden_half:]).astype(bf16)

    hidden_kept = copies_to(hidden, RING, 8).reshape(ROWS, hidden_half)
    hidden_other = swap(hidden_kept)
    down_kept, down_other = halves(down_weight, core, 0)
    mixed = (dot(down_kept, hidden_kept, 0, 1) + dot(down_other, hidden_other, 0, 1)).astype(bf16)
    mixed = jnp.sum(copies_to(mixed, MP, 8).astype(f32), axis=0)
    stream_cols = (source.T + mixed).astype(bf16)

    blocks_kept = copies_to(stream_cols, RING, 8)
    blocks_other = swap(blocks_kept)
    encoder_blocks = encoder_weight.reshape(8, 2, D // 16, -1)
    encoder_kept = jnp.where(core == 0, encoder_blocks[:, 0], encoder_blocks[:, 1]).reshape(HALF, -1)
    encoder_other = jnp.where(core == 0, encoder_blocks[:, 1], encoder_blocks[:, 0]).reshape(HALF, -1)
    encoded = (
        dot(blocks_kept.reshape(HALF, ROWS), encoder_kept, 0, 0)
        + dot(blocks_other.reshape(HALF, ROWS), encoder_other, 0, 0)
        + encoder_bias[None, :]
    )
    codes = jax.nn.softplus(encoded).astype(bf16)

    decoder_kept, decoder_other = halves(decoder_weight, core, 1)
    arrived = swap(dot(codes, decoder_other, 1, 0).astype(bf16))
    both = (dot(codes, decoder_kept, 1, 0) + arrived.astype(f32)).astype(bf16)
    recon = jnp.sum(exchange(both.reshape(CHIPS, 4, HALF), CHIP).astype(f32), axis=0)
    recon = recon + halves(decoder_bias, core, 0)[0][None, :]

    stream = jnp.where(
        core == 0,
        jnp.stack([blocks_kept, blocks_other], axis=1),
        jnp.stack([blocks_other, blocks_kept], axis=1),
    ).reshape(D, ROWS)
    own = chip * 4 + lax.broadcasted_iota(jnp.int32, (4, ROWS), 0)
    own = (lax.broadcasted_iota(jnp.int32, (4, ROWS), 1) == own).astype(bf16)
    stream_own = dot(own, halves(stream, core, 0)[0], 1, 1)

    error = (recon - stream_own).astype(bf16)
    error_kept = copies_to(error, CHIP, CHIPS).reshape(ROWS, HALF)
    error_other = swap(error_kept)
    code_gradient = dot(error_kept, decoder_kept, 1, 1) + dot(error_other, decoder_other, 1, 1)
    encoded_gradient = (jax.nn.sigmoid(encoded) * (code_gradient + sparsity_weight)).astype(bf16)

    top_kept, top_other = halves(encoder_weight, core, 0)
    arrived = swap(dot(encoded_gradient, top_other, 1, 1).astype(bf16))
    both = (dot(encoded_gradient, top_kept, 1, 1) + arrived.astype(f32)).astype(bf16)
    terms = exchange(both.reshape(CHIPS, 4, HALF), CHIP)
    decoder_gradient = dot(codes, joined(error_kept, error_other, 1), 0, 0).astype(bf16)
    encoder_gradient = dot(stream, encoded_gradient, 1, 0).astype(bf16)
    terms, decoder_gradient, encoder_gradient = lax.optimization_barrier(
        (terms, decoder_gradient, encoder_gradient)
    )
    input_gradient = jnp.sum(terms.astype(f32), axis=0) - error.astype(f32)

    def own_rows(v):
        mine, others = halves(v, core, 0)
        return joined(mine, swap(others), 1)

    return codes, own_rows(recon.astype(bf16)), encoder_gradient, decoder_gradient, own_rows(input_gradient)


def solution(mesh):
    fine = Mesh(mesh.devices.reshape(2, 4, 4, 2, 2), ("zl", "x", "y", "zh", "c"))
    in_specs = (
        P(None, FEAT),
        P(FEAT),
        P(FEAT, MP),
        P(FEAT, MP),
        P(MP, FEAT),
        P(None, ALL),
        P(ALL),
        P(ALL, None),
        P(),
    )
    out_specs = (P(None, ALL), P(ALL, None), P(None, ALL), P(ALL, None), P(ALL, None))
    return jax.shard_map(shards, mesh=fine, in_specs=in_specs, out_specs=out_specs, check_vma=False)
```

```python
import jax
import jax.numpy as jnp
from jax import lax
from jax.sharding import Mesh
from jax.sharding import PartitionSpec as P

D = 3584
ROWS = 256
HALF = ROWS // 2
CHIPS = 64

MP = ("zl", "x")
RING = ("y", "zh")
FEAT = RING + ("c",)
CHIP = MP + RING
ALL = MP + FEAT

sparsity_weight = 0.2
norm_eps = 1e-06
bf16 = jnp.bfloat16
f32 = jnp.float32


def dot(a, b, ca, cb):
    return lax.dot_general(a, b, (((ca,), (cb,)), ((), ())), preferred_element_type=f32)


def swap(v):
    return lax.ppermute(v, "c", [(0, 1), (1, 0)])


def exchange(v, axes):
    return lax.all_to_all(v, axes, 0, 0, tiled=True)


def copies_to(v, axes, parts):
    return exchange(jnp.broadcast_to(v[None], (parts,) + v.shape), axes)


def three(v):
    hi = v.astype(bf16)
    mid = (v - hi.astype(f32)).astype(bf16)
    lo = (v - hi.astype(f32) - mid.astype(f32)).astype(bf16)
    return jnp.stack([hi, mid, lo], axis=-1)


def shards(
    residual_in,
    norm_gain,
    gate_weight,
    up_weight,
    down_weight,
    encoder_weight,
    encoder_bias,
    decoder_weight,
    decoder_bias,
):
    hidden_local = gate_weight.shape[1]
    core = lax.axis_index("c")

    def by_core(zero, one):
        return jnp.where(core == 0, zero, one)

    at = lax.broadcasted_iota(jnp.int32, (ROWS, ROWS), 0)
    row = lax.broadcasted_iota(jnp.int32, (ROWS, ROWS), 1)
    inside = at % HALF
    order = (row == (inside // 2) * 4 + (at // HALF) * 2 + inside % 2).astype(bf16)
    keep_order = by_core(order[:HALF], order[HALF:])
    send_order = by_core(order[HALF:], order[:HALF])

    joint_weight = jnp.concatenate([gate_weight, up_weight], axis=1)

    def project(rows):
        source = dot(rows, residual_in, 1, 0)
        squares = jnp.sum(source * source, axis=1)
        return dot((source * norm_gain[None, :]).astype(bf16), joint_weight, 1, 0), squares

    sent, squares_sent = project(send_order)
    arrived, squares_arrived = swap(sent.astype(bf16)), swap(squares_sent)
    kept, squares_kept = project(keep_order)
    both = (kept + arrived.astype(f32)).astype(bf16)
    both = jnp.concatenate([both, jnp.pad(three(squares_kept + squares_arrived), ((0, 0), (0, 125)))], axis=1)
    both = exchange(both.reshape(8, 16, both.shape[1]), RING)
    projected = jnp.sum(both.astype(f32), axis=0)
    mean = jnp.sum(projected[:, 2 * hidden_local :], axis=1, keepdims=True) / D
    projected = projected[:, : 2 * hidden_local] * lax.rsqrt(mean + norm_eps)
    hidden = (jax.nn.silu(projected[:, :hidden_local]) * projected[:, hidden_local:]).astype(bf16)

    hidden_kept = copies_to(hidden, RING, 8).reshape(HALF, hidden_local)
    hidden_other = swap(hidden_kept)
    mixed_kept = dot(down_weight, hidden_kept, 0, 1).astype(bf16)
    mixed_other = dot(down_weight, hidden_other, 0, 1).astype(bf16)
    mixed = by_core(
        jnp.concatenate([mixed_kept, mixed_other], axis=1),
        jnp.concatenate([mixed_other, mixed_kept], axis=1),
    )
    mixed = jnp.sum(copies_to(mixed, MP, 8).astype(f32), axis=0)
    stream_cols = (dot(residual_in, order, 0, 1) + mixed).astype(bf16)

    blocks_kept = copies_to(stream_cols, RING, 8)
    blocks_other = swap(blocks_kept)
    encoder_blocks = encoder_weight.reshape(8, 2, D // 16, -1)
    encoder_kept = by_core(encoder_blocks[:, 0], encoder_blocks[:, 1]).reshape(D // 2, -1)
    encoder_other = by_core(encoder_blocks[:, 1], encoder_blocks[:, 0]).reshape(D // 2, -1)
    encoded = (
        dot(blocks_kept.reshape(D // 2, ROWS), encoder_kept, 0, 0)
        + dot(blocks_other.reshape(D // 2, ROWS), encoder_other, 0, 0)
        + encoder_bias[None, :]
    )
    codes = jax.nn.softplus(encoded).astype(bf16)
    codes_kept = by_core(codes[:HALF], codes[HALF:])
    codes_other = by_core(codes[HALF:], codes[:HALF])

    arrived = swap(dot(codes_other, decoder_weight, 1, 0).astype(bf16))
    both = (dot(codes_kept, decoder_weight, 1, 0) + arrived.astype(f32)).astype(bf16)
    terms = exchange(both.reshape(CHIPS, 2, D), CHIP)
    stream = by_core(
        jnp.stack([blocks_kept, blocks_other], axis=1),
        jnp.stack([blocks_other, blocks_kept], axis=1),
    ).reshape(D, ROWS)
    chip = lax.axis_index(CHIP)
    own = core * HALF + chip * 2 + lax.broadcasted_iota(jnp.int32, (2, ROWS), 0)
    own = (lax.broadcasted_iota(jnp.int32, (2, ROWS), 1) == own).astype(bf16)
    terms, stream, stream_own, codes_out = lax.optimization_barrier(
        (terms, stream, dot(own, stream, 1, 1), dot(order, codes, 0, 0).astype(bf16))
    )
    recon_own = jnp.sum(terms.astype(f32), axis=0) + decoder_bias[None, :]
    error_own = (recon_own - stream_own).astype(bf16)

    error_kept = copies_to(error_own, CHIP, CHIPS).reshape(HALF, D)
    error = jnp.concatenate([error_kept, swap(error_kept)], axis=0)
    slope = jax.nn.sigmoid(encoded)
    slope = by_core(slope, jnp.concatenate([slope[HALF:], slope[:HALF]], axis=0))
    code_gradient = dot(error, decoder_weight, 1, 1)
    grad = (slope * (code_gradient + sparsity_weight)).astype(bf16)
    summed = dot(grad, encoder_weight, 1, 1)
    arrived = swap(summed[HALF:].astype(bf16))
    both = (summed[:HALF] + arrived.astype(f32)).astype(bf16)
    terms = exchange(both.reshape(CHIPS, 2, D), CHIP)

    decoder_gradient = dot(jnp.concatenate([codes_kept, codes_other], axis=0), error, 0, 0).astype(bf16)
    grad = by_core(grad, jnp.concatenate([grad[HALF:], grad[:HALF]], axis=0))
    encoder_gradient = dot(stream, grad, 1, 0).astype(bf16)
    terms, decoder_gradient, encoder_gradient = lax.optimization_barrier(
        (terms, decoder_gradient, encoder_gradient)
    )
    input_gradient = jnp.sum(terms.astype(f32), axis=0) - error_own.astype(f32)
    return codes_out, recon_own.astype(bf16), encoder_gradient, decoder_gradient, input_gradient


def solution(mesh):
    fine = Mesh(mesh.devices.reshape(2, 4, 4, 2, 2), ("zl", "x", "y", "zh", "c"))
    in_specs = (
        P(None, FEAT),
        P(FEAT),
        P(FEAT, MP),
        P(FEAT, MP),
        P(MP, FEAT),
        P(None, ALL),
        P(ALL),
        P(ALL, None),
        P(),
    )
    out_specs = (P(None, ALL), P(ALL, None), P(None, ALL), P(ALL, None), P(ALL, None))
    return jax.shard_map(shards, mesh=fine, in_specs=in_specs, out_specs=out_specs, check_vma=False)
```

```python
import jax
import jax.numpy as jnp
import numpy as np
from jax import lax
from jax.experimental import pallas as pl
from jax.experimental.pallas import tpu as pltpu
from jax.sharding import Mesh
from jax.sharding import PartitionSpec as P

D = 3584
ROWS = 256
HALF = ROWS // 2
CHIPS = 64

MP = ("zl", "x")
RING = ("y", "zh")
FEAT = RING + ("c",)
CHIP = MP + RING
ALL = MP + FEAT

sparsity_weight = 0.2
norm_eps = 1e-06
bf16 = jnp.bfloat16
f32 = jnp.float32


def dot(a, b, ca, cb):
    return lax.dot_general(a, b, (((ca,), (cb,)), ((), ())), preferred_element_type=f32)


def swap(v):
    return lax.ppermute(v, "c", [(0, 1), (1, 0)])


def exchange(v, axes):
    return lax.all_to_all(v, axes, 0, 0, tiled=True)


def copies_to(v, axes, parts):
    return exchange(jnp.broadcast_to(v[None], (parts,) + v.shape), axes)


def local(kernel, outs, ins, flops):
    return pl.pallas_call(
        kernel,
        out_shape=[jax.ShapeDtypeStruct(shape, kind) for shape, kind in outs],
        in_specs=[pl.BlockSpec(memory_space=pltpu.VMEM) for _ in ins],
        out_specs=[pl.BlockSpec(memory_space=pltpu.VMEM) for _ in outs],
        compiler_params=pltpu.CompilerParams(vmem_limit_bytes=12 * 2**20),
        cost_estimate=pl.CostEstimate(flops=flops, bytes_accessed=2**21, transcendentals=0),
    )(*ins)


def three(v):
    first = v.astype(bf16).astype(f32)
    second = (v - first).astype(bf16).astype(f32)
    third = v - first - second
    lane = lax.broadcasted_iota(jnp.int32, v.shape, 1)
    parts = jnp.where(lane == 0, first, jnp.where(lane == 1, second, jnp.where(lane == 2, third, 0.0)))
    return parts.astype(bf16)


def rows_of(core):
    row = lax.broadcasted_iota(jnp.int32, (ROWS, HALF), 0)
    at = lax.broadcasted_iota(jnp.int32, (ROWS, HALF), 1)
    return (row == (at // 2) * 4 + core * 2 + at % 2).astype(bf16)


def scaled_rows(source, gain, picked):
    size = source.shape[0]
    same = lax.broadcasted_iota(jnp.int32, (size, size), 0) == lax.broadcasted_iota(jnp.int32, (size, size), 1)
    column = jnp.sum(jnp.where(same, gain[...], 0.0), axis=1, keepdims=True)
    rows = dot(source[...], picked, 1, 0)
    squared = rows * rows
    high = squared.astype(bf16)
    low = (squared - high.astype(f32)).astype(bf16)
    ones = jnp.ones((size, 128), bf16)
    return (rows * column).astype(bf16), dot(high, ones, 0, 0) + dot(low, ones, 0, 0)


def assemble(kept, other, out):
    core = lax.axis_index("c")
    for k in range(kept.shape[0]):
        out[k, core] = kept[k]
        out[k, 1 - core] = other[k]


def reorder(rows, v, out):
    out[...] = dot(rows[...], v[...], 1, 0).astype(bf16)


def retile(v, out):
    for at in range(0, v.shape[2], 512):
        out[:, at : at + 512] = v[:, :, at : at + 512].astype(f32).reshape(HALF, 512).astype(bf16)


def merge(kept, arrived, out):
    for at in range(0, out.shape[2], 512):
        term = kept[:, at : at + 512] + arrived[:, at : at + 512].astype(f32)
        out[:, :, at : at + 512] = term.reshape(CHIPS, 2, 512).astype(bf16)


def project_other(source, gain, weight, order, sent, ordered):
    ordered[...] = dot(source[...], order[...], 1, 1).astype(bf16)
    scaled, squares = scaled_rows(source, gain, rows_of(1 - lax.axis_index("c")))
    columns = weight.shape[1]
    for at in range(0, columns, 512):
        sent[:, at : at + 512] = dot(scaled, weight[:, at : at + 512], 0, 0).astype(bf16)
    sent[:, columns:] = three(squares)


def project_kept(source, gain, weight, arrived, out):
    scaled, squares = scaled_rows(source, gain, rows_of(lax.axis_index("c")))
    columns = weight.shape[1]
    for at in range(0, columns, 512):
        term = dot(scaled, weight[:, at : at + 512], 0, 0)
        out[:, at : at + 512] = (term + arrived[:, at : at + 512].astype(f32)).astype(bf16)
    out[:, columns:] = three(squares + jnp.sum(arrived[:, columns:].astype(f32), axis=1, keepdims=True))


def shards(
    residual_in,
    norm_gain,
    gate_weight,
    up_weight,
    down_weight,
    encoder_weight,
    encoder_bias,
    decoder_weight,
    decoder_bias,
):
    hidden_local = gate_weight.shape[1]
    core = lax.axis_index("c")
    piece = residual_in.shape[1] // 8
    first_core, piece_at, own_at, residual_in = lax.optimization_barrier(
        (
            core == 0,
            (lax.axis_index(MP) * piece).astype(jnp.uint32),
            core * HALF + lax.axis_index(CHIP) * 2,
            residual_in,
        )
    )

    def by_core(zero, one):
        return jnp.where(first_core, zero, one)

    at = np.arange(ROWS)
    place = (at % HALF) // 2 * 4 + at // HALF * 2 + at % 2
    order = jnp.asarray(np.eye(ROWS)[place], bf16)

    joint_weight = jnp.concatenate([gate_weight, up_weight], axis=1)
    operands = [residual_in.T, norm_gain[None, :], joint_weight]
    payload = [((HALF, joint_weight.shape[1] + 128), bf16)]
    sent, ordered = local(
        project_other,
        payload + [(operands[0].shape, bf16)],
        operands + [order],
        10**9,
    )
    (both,) = local(project_kept, payload, operands + [swap(sent)], 10**9)
    both = exchange(both.reshape(8, 16, both.shape[1]), RING)
    projected = jnp.sum(both.astype(f32), axis=0)
    mean = jnp.sum(projected[:, 2 * hidden_local :], axis=1, keepdims=True) / D
    projected = projected[:, : 2 * hidden_local] * lax.rsqrt(mean + norm_eps)
    hidden = (jax.nn.silu(projected[:, :hidden_local]) * projected[:, hidden_local:]).astype(bf16)

    hidden_kept = copies_to(hidden, RING, 8).reshape(HALF, hidden_local)
    hidden_other = swap(hidden_kept)
    mixed_kept = dot(down_weight, hidden_kept, 0, 1).astype(bf16)
    mixed_other = dot(down_weight, hidden_other, 0, 1).astype(bf16)
    mixed = by_core(
        jnp.concatenate([mixed_kept, mixed_other], axis=1),
        jnp.concatenate([mixed_other, mixed_kept], axis=1),
    )
    mixed = jnp.sum(exchange(mixed.reshape(8, piece, ROWS), MP).astype(f32), axis=0)
    source = lax.dynamic_slice(ordered, (piece_at, jnp.uint32(0)), (piece, ROWS)).astype(f32)
    stream_piece = (source + mixed).astype(bf16)

    blocks_kept = copies_to(stream_piece, RING + MP, CHIPS).reshape(8, 8 * piece, ROWS)
    blocks_kept = lax.optimization_barrier(blocks_kept)
    blocks_other = swap(blocks_kept)
    (stream,) = local(
        assemble, [((8, 2) + blocks_kept.shape[1:], bf16)], [blocks_kept, blocks_other], 10**7
    )
    stream = stream.reshape(D, ROWS)
    encoded = dot(stream, encoder_weight, 0, 0) + encoder_bias[None, :]
    codes = jax.nn.softplus(encoded).astype(bf16)
    codes_kept = by_core(codes[:HALF], codes[HALF:])
    codes_other = by_core(codes[HALF:], codes[:HALF])

    arrived = swap(dot(codes_other, decoder_weight, 1, 0).astype(bf16))
    pieces = [((CHIPS, 2, D), bf16)]
    own = own_at + lax.broadcasted_iota(jnp.int32, (2, ROWS), 0)
    own = (lax.broadcasted_iota(jnp.int32, (2, ROWS), 1) == own).astype(bf16)
    kept, offset = lax.optimization_barrier(
        (dot(codes_kept, decoder_weight, 1, 0), decoder_bias[None, :] - dot(own, stream, 1, 1))
    )
    (both,) = local(merge, pieces, [kept, arrived], 10**7)
    terms = exchange(both, CHIP)
    recon_own = jnp.sum(terms.astype(f32), axis=0)
    error_own = (recon_own + offset).astype(bf16)

    error_kept = copies_to(error_own, CHIP, CHIPS)
    error_other = swap(error_kept)
    (error_kept,) = local(retile, [((HALF, D), bf16)], [error_kept], 10**7)
    slope = jax.nn.sigmoid(encoded)
    slope_kept = by_core(slope[:HALF], slope[HALF:])
    slope_other = by_core(slope[HALF:], slope[:HALF])
    grad_kept = (slope_kept * (dot(error_kept, decoder_weight, 1, 1) + sparsity_weight)).astype(bf16)
    grad_kept, error_other = lax.optimization_barrier((grad_kept, error_other))
    (error_other,) = local(retile, [((HALF, D), bf16)], [error_other], 10**7)
    grad_other = (slope_other * (dot(error_other, decoder_weight, 1, 1) + sparsity_weight)).astype(bf16)
    arrived = swap(dot(grad_other, encoder_weight, 1, 1).astype(bf16))
    (both,) = local(merge, pieces, [dot(grad_kept, encoder_weight, 1, 1), arrived], 10**7)
    both, recon_own, codes, codes_kept, codes_other, error_kept, error_other, grad_kept, grad_other = (
        lax.optimization_barrier(
            (both, recon_own, codes, codes_kept, codes_other, error_kept, error_other, grad_kept, grad_other)
        )
    )
    terms = exchange(both, CHIP)
    recon_own = (recon_own + decoder_bias[None, :]).astype(bf16)
    (codes_out,) = local(
        reorder, [(codes.shape, bf16)], [jnp.asarray(np.eye(ROWS)[place].T, bf16), codes], 10**8
    )
    decoder_gradient = dot(
        jnp.concatenate([codes_kept, codes_other], axis=0),
        jnp.concatenate([error_kept, error_other], axis=0),
        0,
        0,
    ).astype(bf16)
    grad = by_core(
        jnp.concatenate([grad_kept, grad_other], axis=0),
        jnp.concatenate([grad_other, grad_kept], axis=0),
    )
    encoder_gradient = dot(stream, grad, 1, 0).astype(bf16)
    terms, decoder_gradient, encoder_gradient, recon_own, codes_out = lax.optimization_barrier(
        (terms, decoder_gradient, encoder_gradient, recon_own, codes_out)
    )
    input_gradient = jnp.sum(terms.astype(f32), axis=0) - error_own.astype(f32)
    return codes_out, recon_own, encoder_gradient, decoder_gradient, input_gradient


def solution(mesh):
    fine = Mesh(mesh.devices.reshape(2, 4, 4, 2, 2), ("zl", "x", "y", "zh", "c"))
    in_specs = (
        P(None, FEAT),
        P(FEAT),
        P(FEAT, MP),
        P(FEAT, MP),
        P(MP, FEAT),
        P(None, ALL),
        P(ALL),
        P(ALL, None),
        P(),
    )
    out_specs = (P(None, ALL), P(ALL, None), P(None, ALL), P(ALL, None), P(ALL, None))
    return jax.shard_map(shards, mesh=fine, in_specs=in_specs, out_specs=out_specs, check_vma=False)
```

```python
import jax
import jax.numpy as jnp
import numpy as np
from jax import lax
from jax.experimental import pallas as pl
from jax.experimental.pallas import tpu as pltpu
from jax.sharding import Mesh
from jax.sharding import PartitionSpec as P

D = 3584
ROWS = 256
HALF = ROWS // 2
CHIPS = 64

MP = ("zl", "x")
RING = ("y", "zh")
FEAT = RING + ("c",)
CHIP = MP + RING
ALL = MP + FEAT

sparsity_weight = 0.2
norm_eps = 1e-06
bf16 = jnp.bfloat16
f32 = jnp.float32


def dot(a, b, ca, cb):
    return lax.dot_general(a, b, (((ca,), (cb,)), ((), ())), preferred_element_type=f32)


def swap(v):
    return lax.ppermute(v, "c", [(0, 1), (1, 0)])


def exchange(v, axes):
    return lax.all_to_all(v, axes, 0, 0, tiled=True)


def copies_to(v, axes, parts):
    return exchange(jnp.broadcast_to(v[None], (parts,) + v.shape), axes)


def local(kernel, outs, ins, flops):
    return pl.pallas_call(
        kernel,
        out_shape=[jax.ShapeDtypeStruct(shape, kind) for shape, kind in outs],
        in_specs=[pl.BlockSpec(memory_space=pltpu.VMEM) for _ in ins],
        out_specs=[pl.BlockSpec(memory_space=pltpu.VMEM) for _ in outs],
        compiler_params=pltpu.CompilerParams(vmem_limit_bytes=12 * 2**20),
        cost_estimate=pl.CostEstimate(flops=flops, bytes_accessed=2**21, transcendentals=0),
    )(*ins)


def three(v):
    first = v.astype(bf16).astype(f32)
    second = (v - first).astype(bf16).astype(f32)
    third = v - first - second
    lane = lax.broadcasted_iota(jnp.int32, v.shape, 1)
    parts = jnp.where(lane == 0, first, jnp.where(lane == 1, second, jnp.where(lane == 2, third, 0.0)))
    return parts.astype(bf16)


def rows_of(core):
    row = lax.broadcasted_iota(jnp.int32, (ROWS, HALF), 0)
    at = lax.broadcasted_iota(jnp.int32, (ROWS, HALF), 1)
    return (row == (at // 2) * 4 + core * 2 + at % 2).astype(bf16)


def assemble(kept, other, out):
    core = lax.axis_index("c")
    for k in range(kept.shape[0]):
        out[k, core] = kept[k]
        out[k, 1 - core] = other[k]


def reorder(rows, v, out):
    out[...] = dot(rows[...], v[...], 1, 0).astype(bf16)


def retile(v, out):
    for at in range(0, v.shape[2], 512):
        out[:, at : at + 512] = v[:, :, at : at + 512].astype(f32).reshape(HALF, 512).astype(bf16)


def merge(kept, arrived, out):
    for at in range(0, out.shape[2], 512):
        term = kept[:, at : at + 512] + arrived[:, at : at + 512].astype(f32)
        out[:, :, at : at + 512] = term.reshape(CHIPS, 2, 512).astype(bf16)


def square_sums(rows):
    squared = rows * rows
    high = squared.astype(bf16)
    low = (squared - high.astype(f32)).astype(bf16)
    ones = jnp.ones((rows.shape[0], 128), bf16)
    return dot(high, ones, 0, 0) + dot(low, ones, 0, 0)


def project_other(source, gain, weight, sent, ordered, scaled, squares):
    size = source.shape[0]
    same = lax.broadcasted_iota(jnp.int32, (size, size), 0) == lax.broadcasted_iota(jnp.int32, (size, size), 1)
    column = jnp.sum(jnp.where(same, gain[...], 0.0), axis=1, keepdims=True)
    zero, one = dot(source[...], rows_of(0), 1, 0), dot(source[...], rows_of(1), 1, 0)
    ordered[:, :HALF] = zero.astype(bf16)
    ordered[:, HALF:] = one.astype(bf16)
    first = lax.axis_index("c") == 0
    kept, other = jnp.where(first, zero, one), jnp.where(first, one, zero)
    scaled[...] = (kept * column).astype(bf16)
    squares[...] = square_sums(kept)
    other_scaled = (other * column).astype(bf16)
    columns = weight.shape[1]
    for at in range(0, columns, 512):
        sent[:, at : at + 512] = dot(other_scaled, weight[:, at : at + 512], 0, 0).astype(bf16)
    sent[:, columns:] = three(square_sums(other))


def project_kept(scaled, squares, weight, arrived, out):
    columns = weight.shape[1]
    for at in range(0, columns, 512):
        term = dot(scaled[...], weight[:, at : at + 512], 0, 0)
        out[:, at : at + 512] = (term + arrived[:, at : at + 512].astype(f32)).astype(bf16)
    more = jnp.sum(arrived[:, columns:].astype(f32), axis=1, keepdims=True)
    out[:, columns:] = three(squares[...] + more)


def shards(
    residual_in,
    norm_gain,
    gate_weight,
    up_weight,
    down_weight,
    encoder_weight,
    encoder_bias,
    decoder_weight,
    decoder_bias,
):
    hidden_local = gate_weight.shape[1]
    core = lax.axis_index("c")
    piece = residual_in.shape[1] // 8
    first_core, piece_at, own_at, residual_in = lax.optimization_barrier(
        (
            core == 0,
            (lax.axis_index(MP) * piece).astype(jnp.uint32),
            core * HALF + lax.axis_index(CHIP) * 2,
            residual_in,
        )
    )

    def by_core(zero, one):
        return jnp.where(first_core, zero, one)

    at = np.arange(ROWS)
    place = (at % HALF) // 2 * 4 + at // HALF * 2 + at % 2
    joint_weight = jnp.concatenate([gate_weight, up_weight], axis=1)
    payload = [((HALF, joint_weight.shape[1] + 128), bf16)]
    columns = residual_in.shape[1]
    sent, ordered, scaled, squares = local(
        project_other,
        payload + [((columns, ROWS), bf16), ((columns, HALF), bf16), ((HALF, 128), f32)],
        [residual_in.T, norm_gain[None, :], joint_weight],
        10**9,
    )
    (both,) = local(project_kept, payload, [scaled, squares, joint_weight, swap(sent)], 10**9)
    both = exchange(both.reshape(8, 16, both.shape[1]), RING)
    projected = jnp.sum(both.astype(f32), axis=0)
    mean = jnp.sum(projected[:, 2 * hidden_local :], axis=1, keepdims=True) / D
    projected = projected[:, : 2 * hidden_local] * lax.rsqrt(mean + norm_eps)
    hidden = (jax.nn.silu(projected[:, :hidden_local]) * projected[:, hidden_local:]).astype(bf16)

    hidden_kept = copies_to(hidden, RING, 8).reshape(HALF, hidden_local)
    hidden_other = swap(hidden_kept)
    mixed_kept = dot(down_weight, hidden_kept, 0, 1).astype(bf16)
    mixed_other = dot(down_weight, hidden_other, 0, 1).astype(bf16)
    mixed = by_core(
        jnp.concatenate([mixed_kept, mixed_other], axis=1),
        jnp.concatenate([mixed_other, mixed_kept], axis=1),
    )
    mixed = jnp.sum(exchange(mixed.reshape(8, piece, ROWS), MP).astype(f32), axis=0)
    source = lax.dynamic_slice(ordered, (piece_at, jnp.uint32(0)), (piece, ROWS)).astype(f32)
    stream_piece = (source + mixed).astype(bf16)

    blocks_kept = copies_to(stream_piece, RING + MP, CHIPS).reshape(8, 8 * piece, ROWS)
    blocks_kept = lax.optimization_barrier(blocks_kept)
    blocks_other = swap(blocks_kept)
    (stream,) = local(
        assemble, [((8, 2) + blocks_kept.shape[1:], bf16)], [blocks_kept, blocks_other], 10**7
    )
    stream = stream.reshape(D, ROWS)
    encoded = dot(stream, encoder_weight, 0, 0) + encoder_bias[None, :]
    codes = jax.nn.softplus(encoded).astype(bf16)
    codes_kept = by_core(codes[:HALF], codes[HALF:])
    codes_other = by_core(codes[HALF:], codes[:HALF])

    arrived = swap(dot(codes_other, decoder_weight, 1, 0).astype(bf16))
    pieces = [((CHIPS, 2, D), bf16)]
    own = own_at + lax.broadcasted_iota(jnp.int32, (2, ROWS), 0)
    own = (lax.broadcasted_iota(jnp.int32, (2, ROWS), 1) == own).astype(bf16)
    kept, offset = lax.optimization_barrier(
        (dot(codes_kept, decoder_weight, 1, 0), decoder_bias[None, :] - dot(own, stream, 1, 1))
    )
    (both,) = local(merge, pieces, [kept, arrived], 10**7)
    terms = exchange(both, CHIP)
    recon_own = jnp.sum(terms.astype(f32), axis=0)
    error_own = (recon_own + offset).astype(bf16)

    error_kept = copies_to(error_own, CHIP, CHIPS)
    error_other = swap(error_kept)
    (error_kept,) = local(retile, [((HALF, D), bf16)], [error_kept], 10**7)
    slope = jax.nn.sigmoid(encoded)
    slope_kept = by_core(slope[:HALF], slope[HALF:])
    slope_other = by_core(slope[HALF:], slope[:HALF])
    grad_kept = (slope_kept * (dot(error_kept, decoder_weight, 1, 1) + sparsity_weight)).astype(bf16)
    grad_kept, error_other = lax.optimization_barrier((grad_kept, error_other))
    (error_other,) = local(retile, [((HALF, D), bf16)], [error_other], 10**7)
    grad_other = (slope_other * (dot(error_other, decoder_weight, 1, 1) + sparsity_weight)).astype(bf16)
    arrived = swap(dot(grad_other, encoder_weight, 1, 1).astype(bf16))
    (both,) = local(merge, pieces, [dot(grad_kept, encoder_weight, 1, 1), arrived], 10**7)
    both, recon_own, codes, codes_kept, codes_other, error_kept, error_other, grad_kept, grad_other = (
        lax.optimization_barrier(
            (both, recon_own, codes, codes_kept, codes_other, error_kept, error_other, grad_kept, grad_other)
        )
    )
    terms = exchange(both, CHIP)
    recon_own = (recon_own + decoder_bias[None, :]).astype(bf16)
    (codes_out,) = local(
        reorder, [(codes.shape, bf16)], [jnp.asarray(np.eye(ROWS)[place].T, bf16), codes], 10**8
    )
    decoder_gradient = dot(
        jnp.concatenate([codes_kept, codes_other], axis=0),
        jnp.concatenate([error_kept, error_other], axis=0),
        0,
        0,
    ).astype(bf16)
    grad = by_core(
        jnp.concatenate([grad_kept, grad_other], axis=0),
        jnp.concatenate([grad_other, grad_kept], axis=0),
    )
    encoder_gradient = dot(stream, grad, 1, 0).astype(bf16)
    terms, decoder_gradient, encoder_gradient, recon_own, codes_out = lax.optimization_barrier(
        (terms, decoder_gradient, encoder_gradient, recon_own, codes_out)
    )
    input_gradient = jnp.sum(terms.astype(f32), axis=0) - error_own.astype(f32)
    return codes_out, recon_own, encoder_gradient, decoder_gradient, input_gradient


def solution(mesh):
    fine = Mesh(mesh.devices.reshape(2, 4, 4, 2, 2), ("zl", "x", "y", "zh", "c"))
    in_specs = (
        P(None, FEAT),
        P(FEAT),
        P(FEAT, MP),
        P(FEAT, MP),
        P(MP, FEAT),
        P(None, ALL),
        P(ALL),
        P(ALL, None),
        P(),
    )
    out_specs = (P(None, ALL), P(ALL, None), P(None, ALL), P(ALL, None), P(ALL, None))
    return jax.shard_map(shards, mesh=fine, in_specs=in_specs, out_specs=out_specs, check_vma=False)
```

```python
import jax
import jax.numpy as jnp
import numpy as np
from jax import lax
from jax.experimental import pallas as pl
from jax.experimental.pallas import tpu as pltpu
from jax.sharding import Mesh
from jax.sharding import PartitionSpec as P

D = 3584
ROWS = 256
HALF = ROWS // 2
CHIPS = 64

MP = ("zl", "x")
RING = ("y", "zh")
FEAT = RING + ("c",)
CHIP = MP + RING
ALL = MP + FEAT

sparsity_weight = 0.2
norm_eps = 1e-06
bf16 = jnp.bfloat16
f32 = jnp.float32


def dot(a, b, ca, cb):
    return lax.dot_general(a, b, (((ca,), (cb,)), ((), ())), preferred_element_type=f32)


def swap(v):
    return lax.ppermute(v, "c", [(0, 1), (1, 0)])


def exchange(v, axes):
    return lax.all_to_all(v, axes, 0, 0, tiled=True)


def copies_to(v, axes, parts):
    return exchange(jnp.broadcast_to(v[None], (parts,) + v.shape), axes)


def local(kernel, outs, ins, flops):
    return pl.pallas_call(
        kernel,
        out_shape=[jax.ShapeDtypeStruct(shape, kind) for shape, kind in outs],
        in_specs=[pl.BlockSpec(memory_space=pltpu.VMEM) for _ in ins],
        out_specs=[pl.BlockSpec(memory_space=pltpu.VMEM) for _ in outs],
        compiler_params=pltpu.CompilerParams(vmem_limit_bytes=12 * 2**20),
        cost_estimate=pl.CostEstimate(flops=flops, bytes_accessed=2**21, transcendentals=0),
    )(*ins)


def three(v):
    first = v.astype(bf16).astype(f32)
    second = (v - first).astype(bf16).astype(f32)
    third = v - first - second
    lane = lax.broadcasted_iota(jnp.int32, v.shape, 1)
    parts = jnp.where(lane == 0, first, jnp.where(lane == 1, second, jnp.where(lane == 2, third, 0.0)))
    return parts.astype(bf16)


def rows_of(core):
    row = lax.broadcasted_iota(jnp.int32, (ROWS, HALF), 0)
    at = lax.broadcasted_iota(jnp.int32, (ROWS, HALF), 1)
    return (row == (at // 2) * 4 + core * 2 + at % 2).astype(bf16)


def assemble(kept, other, out):
    core = lax.axis_index("c")
    for k in range(kept.shape[0]):
        out[k, core] = kept[k]
        out[k, 1 - core] = other[k]


def reorder(rows, v, out):
    out[...] = dot(rows[...], v[...], 1, 0).astype(bf16)


def retile(v, out):
    for at in range(0, v.shape[2], 512):
        out[:, at : at + 512] = v[:, :, at : at + 512].astype(f32).reshape(HALF, 512).astype(bf16)


def merge(kept, arrived, out):
    for at in range(0, out.shape[2], 512):
        term = kept[:, at : at + 512] + arrived[:, at : at + 512].astype(f32)
        out[:, :, at : at + 512] = term.reshape(CHIPS, 2, 512).astype(bf16)


def square_sums(rows):
    squared = rows * rows
    high = squared.astype(bf16)
    low = (squared - high.astype(f32)).astype(bf16)
    ones = jnp.ones((rows.shape[0], 128), bf16)
    return dot(high, ones, 0, 0) + dot(low, ones, 0, 0)


def project_other(source, weight, sent, ordered, scaled, squares):
    zero, one = dot(source[...], rows_of(0), 1, 0), dot(source[...], rows_of(1), 1, 0)
    ordered[:, :HALF] = zero.astype(bf16)
    ordered[:, HALF:] = one.astype(bf16)
    first = lax.axis_index("c") == 0
    kept, other = jnp.where(first, zero, one), jnp.where(first, one, zero)
    scaled[...] = kept.astype(bf16)
    squares[...] = square_sums(kept)
    other_scaled = other.astype(bf16)
    columns = weight.shape[1]
    for at in range(0, columns, 512):
        sent[:, at : at + 512] = dot(other_scaled, weight[:, at : at + 512], 0, 0).astype(bf16)
    sent[:, columns:] = three(square_sums(other))


def project_kept(scaled, squares, weight, arrived, out):
    columns = weight.shape[1]
    for at in range(0, columns, 512):
        term = dot(scaled[...], weight[:, at : at + 512], 0, 0)
        out[:, at : at + 512] = (term + arrived[:, at : at + 512].astype(f32)).astype(bf16)
    more = jnp.sum(arrived[:, columns:].astype(f32), axis=1, keepdims=True)
    out[:, columns:] = three(squares[...] + more)


def shards(
    residual_in,
    norm_gain,
    gate_weight,
    up_weight,
    down_weight,
    encoder_weight,
    encoder_bias,
    decoder_weight,
    decoder_bias,
):
    hidden_local = gate_weight.shape[1]
    core = lax.axis_index("c")
    piece = residual_in.shape[1] // 8
    first_core, piece_at, own_at, residual_in = lax.optimization_barrier(
        (
            core == 0,
            (lax.axis_index(MP) * piece).astype(jnp.uint32),
            core * HALF + lax.axis_index(CHIP) * 2,
            residual_in,
        )
    )

    def by_core(zero, one):
        return jnp.where(first_core, zero, one)

    at = np.arange(ROWS)
    place = (at % HALF) // 2 * 4 + at // HALF * 2 + at % 2
    gain = norm_gain[:, None]
    joint_weight = jnp.concatenate(
        [(w.astype(f32) * gain).astype(bf16) for w in (gate_weight, up_weight)], axis=1
    )
    payload = [((HALF, joint_weight.shape[1] + 128), bf16)]
    columns = residual_in.shape[1]
    sent, ordered, scaled, squares = local(
        project_other,
        payload + [((columns, ROWS), bf16), ((columns, HALF), bf16), ((HALF, 128), f32)],
        [residual_in.T, joint_weight],
        10**9,
    )
    (both,) = local(project_kept, payload, [scaled, squares, joint_weight, swap(sent)], 10**9)
    both = exchange(both.reshape(8, 16, both.shape[1]), RING)
    projected = jnp.sum(both.astype(f32), axis=0)
    mean = jnp.sum(projected[:, 2 * hidden_local :], axis=1, keepdims=True) / D
    projected = projected[:, : 2 * hidden_local] * lax.rsqrt(mean + norm_eps)
    hidden = (jax.nn.silu(projected[:, :hidden_local]) * projected[:, hidden_local:]).astype(bf16)

    hidden_kept = copies_to(hidden, RING, 8).reshape(HALF, hidden_local)
    hidden_other = swap(hidden_kept)
    mixed_kept = dot(down_weight, hidden_kept, 0, 1).astype(bf16)
    mixed_other = dot(down_weight, hidden_other, 0, 1).astype(bf16)
    mixed = by_core(
        jnp.concatenate([mixed_kept, mixed_other], axis=1),
        jnp.concatenate([mixed_other, mixed_kept], axis=1),
    )
    mixed = jnp.sum(exchange(mixed.reshape(8, piece, ROWS), MP).astype(f32), axis=0)
    source = lax.dynamic_slice(ordered, (piece_at, jnp.uint32(0)), (piece, ROWS)).astype(f32)
    stream_piece = (source + mixed).astype(bf16)

    blocks_kept = copies_to(stream_piece, RING + MP, CHIPS).reshape(8, 8 * piece, ROWS)
    blocks_kept = lax.optimization_barrier(blocks_kept)
    blocks_other = swap(blocks_kept)
    (stream,) = local(
        assemble, [((8, 2) + blocks_kept.shape[1:], bf16)], [blocks_kept, blocks_other], 10**7
    )
    stream = stream.reshape(D, ROWS)
    encoded = dot(stream, encoder_weight, 0, 0) + encoder_bias[None, :]
    codes = jax.nn.softplus(encoded).astype(bf16)
    codes_kept = by_core(codes[:HALF], codes[HALF:])
    codes_other = by_core(codes[HALF:], codes[:HALF])

    arrived = swap(dot(codes_other, decoder_weight, 1, 0).astype(bf16))
    pieces = [((CHIPS, 2, D), bf16)]
    own = own_at + lax.broadcasted_iota(jnp.int32, (2, ROWS), 0)
    own = (lax.broadcasted_iota(jnp.int32, (2, ROWS), 1) == own).astype(bf16)
    kept, offset = lax.optimization_barrier(
        (dot(codes_kept, decoder_weight, 1, 0), decoder_bias[None, :] - dot(own, stream, 1, 1))
    )
    (both,) = local(merge, pieces, [kept, arrived], 10**7)
    terms = exchange(both, CHIP)
    recon_own = jnp.sum(terms.astype(f32), axis=0)
    error_own = (recon_own + offset).astype(bf16)

    error_kept = copies_to(error_own, CHIP, CHIPS)
    error_other = swap(error_kept)
    (error_kept,) = local(retile, [((HALF, D), bf16)], [error_kept], 10**7)
    slope = jax.nn.sigmoid(encoded)
    slope_kept = by_core(slope[:HALF], slope[HALF:])
    slope_other = by_core(slope[HALF:], slope[:HALF])
    grad_kept = (slope_kept * (dot(error_kept, decoder_weight, 1, 1) + sparsity_weight)).astype(bf16)
    grad_kept, error_other = lax.optimization_barrier((grad_kept, error_other))
    (error_other,) = local(retile, [((HALF, D), bf16)], [error_other], 10**7)
    grad_other = (slope_other * (dot(error_other, decoder_weight, 1, 1) + sparsity_weight)).astype(bf16)
    arrived = swap(dot(grad_other, encoder_weight, 1, 1).astype(bf16))
    (both,) = local(merge, pieces, [dot(grad_kept, encoder_weight, 1, 1), arrived], 10**7)
    both, recon_own, codes, codes_kept, codes_other, error_kept, error_other, grad_kept, grad_other = (
        lax.optimization_barrier(
            (both, recon_own, codes, codes_kept, codes_other, error_kept, error_other, grad_kept, grad_other)
        )
    )
    terms = exchange(both, CHIP)
    recon_own = (recon_own + decoder_bias[None, :]).astype(bf16)
    (codes_out,) = local(
        reorder, [(codes.shape, bf16)], [jnp.asarray(np.eye(ROWS)[place].T, bf16), codes], 10**8
    )
    decoder_gradient = dot(
        jnp.concatenate([codes_kept, codes_other], axis=0),
        jnp.concatenate([error_kept, error_other], axis=0),
        0,
        0,
    ).astype(bf16)
    grad = by_core(
        jnp.concatenate([grad_kept, grad_other], axis=0),
        jnp.concatenate([grad_other, grad_kept], axis=0),
    )
    encoder_gradient = dot(stream, grad, 1, 0).astype(bf16)
    terms, decoder_gradient, encoder_gradient, recon_own, codes_out = lax.optimization_barrier(
        (terms, decoder_gradient, encoder_gradient, recon_own, codes_out)
    )
    input_gradient = jnp.sum(terms.astype(f32), axis=0) - error_own.astype(f32)
    return codes_out, recon_own, encoder_gradient, decoder_gradient, input_gradient


def solution(mesh):
    fine = Mesh(mesh.devices.reshape(2, 4, 4, 2, 2), ("zl", "x", "y", "zh", "c"))
    in_specs = (
        P(None, FEAT),
        P(FEAT),
        P(FEAT, MP),
        P(FEAT, MP),
        P(MP, FEAT),
        P(None, ALL),
        P(ALL),
        P(ALL, None),
        P(),
    )
    out_specs = (P(None, ALL), P(ALL, None), P(None, ALL), P(ALL, None), P(ALL, None))
    return jax.shard_map(shards, mesh=fine, in_specs=in_specs, out_specs=out_specs, check_vma=False)
```
